512 devices in a mesh: grp: 4 (over y), comp: 16 (over z_hi, x, core), tp: 8 (over z_lo).
Axes of the slice: x: 4, y: 4, z: 16 (z_hi: 2, z_lo: 8; z = z_hi * 8 + z_lo), core: 2. Of those that a mesh axis runs over, the one named last changes fastest.
Arguments:
- queries: bfloat16 [16384, 8192], P(('grp', 'comp'), 'tp'), parts along dimension 0, may hold values from -18 to 18
- comp_keys: bfloat16 [16384, 1024], P(('grp', 'comp'), 'tp'), parts along dimension 0, may hold values from -6 to 6
- comp_values: bfloat16 [16384, 1024], P(('grp', 'comp'), 'tp'), parts along dimension 0, may hold values from -6 to 6
- prompt_keys: bfloat16 [6144, 1024], P(('grp', 'comp'), 'tp'), parts along dimension 0, may hold values from -16 to 16
- prompt_values: bfloat16 [6144, 1024], P(('grp', 'comp'), 'tp'), parts along dimension 0, may hold values from -6 to 6
- upstream: bfloat16 [16384, 8192], P(('grp', 'comp'), 'tp'), parts along dimension 0, may hold values from -48 to 48
- rewards: float32 [64], P(('grp', 'comp')), parts along dimension 0, may hold values from 0 to 3
- lengths: int32 [64], P(('grp', 'comp')), parts along dimension 0, may hold values from 128 to 256, as said below
Outputs:
- query_grad: bfloat16 [16384, 8192], P(('grp', 'comp'), 'tp'), parts along dimension 0
- comp_key_grad: bfloat16 [16384, 1024], P(('grp', 'comp'), 'tp'), parts along dimension 0
- comp_value_grad: bfloat16 [16384, 1024], P(('grp', 'comp'), 'tp'), parts along dimension 0
- prompt_key_grad: bfloat16 [6144, 1024], P(('grp', 'comp'), 'tp'), parts along dimension 0
- prompt_value_grad: bfloat16 [6144, 1024], P(('grp', 'comp'), 'tp'), parts along dimension 0
The draws below stay inside these ranges and needn't reach their ends.
There are 4 independent parts, one for each index of `grp`. The reference program is written for one: setup_inputs(seed, part) draws one part's arguments, and reference() takes and returns one part's arrays. A program takes and returns all parts, laid end to end along the dimension named above; each array names one. Nothing has to cross between parts.
Inputs may be any that keep to these rules, and one draw needn't show every extreme that they name: lengths are multiples of 128; in every group one completion has all 256 slots valid.
All inputs are finite; a program needn't handle non-finite values.
Results may differ from the reference program's by a relative error of at most 0.0061.
Values may be sent and summed in bfloat16 or wider, within the bound.
A program may use at most 64 MiB of HBM per device.

```python
import math
import jax
import jax.numpy as jnp
from jax import lax

HEADS = 64
KV_HEADS = 8
D_HEAD = 128
COMP_LEN = 256
BLOCK = 128
GROUP = 16
PROMPT = 1536


def draw_queries(key, part):
    key = jax.random.fold_in(key, 1)
    total_rows = GROUP * COMP_LEN
    drawn = jnp.clip(jax.random.normal(key, (total_rows, HEADS * D_HEAD), jnp.float32), -6.0, 6.0)
    return drawn.astype(jnp.bfloat16)


def draw_prompt_keys(key, part):
    key = jax.random.fold_in(key, 2)
    first, second = jax.random.split(key)
    width = KV_HEADS * D_HEAD
    row_scale = jnp.exp(jax.random.uniform(second, (PROMPT, 1), jnp.float32, math.log(0.3), math.log(3.0)))
    drawn = jnp.clip(jax.random.normal(first, (PROMPT, width), jnp.float32), -5.0, 5.0) * row_scale
    return drawn.astype(jnp.bfloat16)


def draw_rewards(key, part):
    key = jax.random.fold_in(key, 3)
    rise = 1.0 + 2.0 * jnp.arange(GROUP, dtype=jnp.float32) / (GROUP - 1)
    base = jax.random.uniform(key, (GROUP,), jnp.float32, 0.5, 1.0)
    return (rise * base).astype(jnp.float32)


def draw_lengths(key, part):
    key = jax.random.fold_in(key, 4)
    first, second = jax.random.split(key)
    counts = jax.random.randint(first, (GROUP,), 1, COMP_LEN // BLOCK + 1)
    full = jax.random.randint(second, (), 0, GROUP)
    counts = jnp.where(jnp.arange(GROUP) == full, COMP_LEN // BLOCK, counts)
    return (counts * BLOCK).astype(jnp.int32)


def steps_of(rng, dims, cuts, smallest, high):
    loudness, own = 1.0, jax.random.fold_in(rng, 6)
    for dim, blocks in cuts:
        steps = jnp.exp(jax.random.uniform(jax.random.fold_in(own, dim), (blocks,), jnp.float32, smallest / len(cuts), high / len(cuts)))
        loudness = loudness * jnp.repeat(steps, dims[dim] // blocks).reshape([-1 if axis == dim else 1 for axis in range(len(dims))])
    return loudness


def bell_draw(rng, dims, spread, reach, cuts=(), kind=jnp.bfloat16):
    factor_of = steps_of(rng, dims, cuts, -0.22, 0.18) if cuts else 1.0
    values = jax.random.normal(rng, dims, jnp.float32) * spread * factor_of
    return jnp.minimum(jnp.maximum(values, -reach), reach).astype(kind)


def setup_inputs(seed: int = 0, part: int = 0) -> dict:
    seeds = jax.random.split(jax.random.key(seed), 9)
    part_splits = jax.random.split(jax.random.fold_in(seeds[8], part), 9)
    return {
        "queries": draw_queries(jax.random.fold_in(jax.random.fold_in(seeds[8], part), 71), part),
        "comp_keys": bell_draw(part_splits[1], (GROUP * COMP_LEN, KV_HEADS * D_HEAD), 1.0, 6.0, ((0, 16), (1, 8))),
        "comp_values": bell_draw(part_splits[2], (GROUP * COMP_LEN, KV_HEADS * D_HEAD), 1.0, 6.0, ((0, 16), (1, 8))),
        "prompt_keys": draw_prompt_keys(jax.random.fold_in(jax.random.fold_in(seeds[8], part), 71), part),
        "prompt_values": bell_draw(part_splits[4], (PROMPT, KV_HEADS * D_HEAD), 1.0, 6.0, ((0, 16), (1, 8))),
        "upstream": bell_draw(part_splits[5], (GROUP * COMP_LEN, HEADS * D_HEAD), 8.0, 48.0, ((0, 16), (1, 8))),
        "rewards": draw_rewards(jax.random.fold_in(jax.random.fold_in(seeds[8], part), 71), part),
        "lengths": draw_lengths(jax.random.fold_in(jax.random.fold_in(seeds[8], part), 71), part),
    }


NEG = -1.0e30


def split_heads(block, groups):
    rows = block.shape[0]
    return block.reshape(rows, groups, -1, D_HEAD).transpose(1, 2, 0, 3)


def split_kv(block, groups):
    rows = block.shape[0]
    return block.reshape(rows, groups, D_HEAD).transpose(1, 0, 2)


def join_kv(block):
    groups, rows, width = block.shape
    return block.transpose(1, 0, 2).reshape(rows, groups * width)


def head_terms(query_head, cot_head, keys, values, keep):
    scale = D_HEAD ** -0.5
    scores = jnp.dot(query_head, keys.T, preferred_element_type=jnp.float32) * scale
    scores = jnp.where(keep, scores, NEG)
    top = jnp.max(scores, axis=1, keepdims=True)
    lse = top + jnp.log(jnp.sum(jnp.exp(scores - top), axis=1, keepdims=True))
    probs = jnp.exp(scores - lse)
    probs_half = probs.astype(jnp.bfloat16)
    attended = jnp.dot(probs_half, values, preferred_element_type=jnp.float32).astype(jnp.bfloat16)
    attended = lax.optimization_barrier(attended)
    delta = jnp.sum(cot_head.astype(jnp.float32) * attended.astype(jnp.float32), axis=1, keepdims=True)
    dprobs = jnp.dot(cot_head, values.T, preferred_element_type=jnp.float32)
    dscores = (probs * (dprobs - delta)).astype(jnp.bfloat16)
    return lse, delta, probs_half, dscores


def attend(query, cot, comp_k, comp_v, prompt_k, prompt_v, first):
    scale = D_HEAD ** -0.5
    groups = comp_k.shape[1] // D_HEAD
    rows = query.shape[0]
    span = prompt_k.shape[0]
    keys = jnp.concatenate([prompt_k, comp_k], 0)
    values = jnp.concatenate([prompt_v, comp_v], 0)
    row_pos = lax.broadcasted_iota(jnp.int32, (rows, span + rows), 0)
    col_pos = lax.broadcasted_iota(jnp.int32, (rows, span + rows), 1)
    keep = (col_pos < span) | (col_pos - span <= row_pos)

    def one_group(operands):
        query_group, cot_group, key_group, value_group = operands

        def one_head(totals, pair):
            query_head, cot_head = pair
            lse, delta, probs_half, dscores = head_terms(query_head, cot_head, key_group, value_group, keep)
            dquery = jnp.dot(dscores, key_group, preferred_element_type=jnp.float32) * scale
            dkey = jnp.dot(dscores[:, first:].T, query_head, preferred_element_type=jnp.float32) * scale
            dvalue = jnp.dot(probs_half[:, first:].T, cot_head, preferred_element_type=jnp.float32)
            return (totals[0] + dkey, totals[1] + dvalue), (dquery, lse, delta)

        empty = jnp.zeros((span + rows - first, D_HEAD), jnp.float32)
        (dkey, dvalue), (dquery, lse, delta) = lax.scan(one_head, (empty, empty), (query_group, cot_group))
        return dkey, dvalue, dquery, lse, delta

    dkey, dvalue, dquery, lse, delta = lax.map(one_group, (split_heads(query, groups), split_heads(cot, groups), split_kv(keys, groups), split_kv(values, groups)))
    dquery = dquery.transpose(2, 0, 1, 3).reshape(rows, -1)
    return dquery, join_kv(dkey), join_kv(dvalue), lse, delta


def reference(queries, comp_keys, comp_values, prompt_keys, prompt_values, upstream, rewards, lengths):
    advantage = rewards - jnp.sum(rewards) / GROUP
    positions = jnp.arange(COMP_LEN, dtype=jnp.int32)
    span = prompt_keys.shape[0]

    def one_completion(totals, index):
        start = (index * COMP_LEN).astype(jnp.int32)
        query = lax.dynamic_slice_in_dim(queries, start, COMP_LEN, 0)
        grad_in = lax.dynamic_slice_in_dim(upstream, start, COMP_LEN, 0)
        comp_k = lax.dynamic_slice_in_dim(comp_keys, start, COMP_LEN, 0)
        comp_v = lax.dynamic_slice_in_dim(comp_values, start, COMP_LEN, 0)
        cot = jnp.where((positions < lengths[index])[:, None], grad_in, jnp.zeros_like(grad_in))
        dquery, dkey, dvalue, lse, delta = attend(query, cot, comp_k, comp_v, prompt_keys, prompt_values, 0)
        weight = advantage[index]
        outs = ((weight * dquery).astype(jnp.bfloat16), (weight * dkey[span:]).astype(jnp.bfloat16), (weight * dvalue[span:]).astype(jnp.bfloat16))
        return (totals[0] + weight * dkey[:span], totals[1] + weight * dvalue[:span]), outs

    empty = jnp.zeros((span, prompt_keys.shape[1]), jnp.float32)
    (key_sum, value_sum), (dq, dck, dcv) = lax.scan(one_completion, (empty, empty), jnp.arange(GROUP, dtype=jnp.int32))
    return (dq.reshape(GROUP * COMP_LEN, -1), dck.reshape(GROUP * COMP_LEN, -1), dcv.reshape(GROUP * COMP_LEN, -1), key_sum.astype(jnp.bfloat16), value_sum.astype(jnp.bfloat16))
```

```python
import math

import jax
import jax.numpy as jnp
from jax import lax
from jax.experimental import pallas as pl
from jax.experimental.pallas import tpu as pltpu
from jax.sharding import PartitionSpec as P

D = 128
HEADS = 8
ROWS = 256
SHARD = 96
PAIR = 2 * SHARD
HALF = 8 * SHARD
SPAN = 2 * HALF
KEYS = SPAN + ROWS
COLS = HEADS * ROWS
CHUNKS = SPAN // PAIR + 1
SCALE = D ** (-0.5)
EXP2_SCALE = SCALE * math.log2(math.e)
F32 = jnp.float32
BF16 = jnp.bfloat16
MESH = pl.DeviceIdType.MESH
NEAR = [(dx, dc) for dx in (2, 1, 3, 0) for dc in (0, 1) if (dx, dc) != (0, 0)]


def slot_of(dx, dc):
    return (dx % 4) * 2 + dc


def mm(a, b):
    return jnp.dot(a, b, preferred_element_type=F32)


def mm_t(a, b):
    return lax.dot_general(a, b, (((1,), (1,)), ((), ())), preferred_element_type=F32)


def kernel(
    q_hbm, ck_hbm, cv_hbm, pk_hbm, pv_hbm, up_hbm, reward_ref, length_ref,
    dq_hbm, dck_hbm, dcv_hbm, dpk_hbm, dpv_hbm,
    q_in, up_in, ck_in, cv_in, pk_in, pv_in,
    dq_out, dck_out, dcv_out, dpk_out, dpv_out,
    qs, cs, kv, kt, exps, dps, ps, dss, tops, sums, dots, factors, deltas,
    own, far_send, far_recv, near_send, near_recv, z_send, z_recv,
    reward_own, reward_z, reward_pair, reward_recv,
    in_sem, out_sem, near_ss, near_rs, far_ss, far_rs, zkv_ss, zkv_rs,
    rfar_ss, rfar_rs, rnear_ss, rnear_rs, rz_ss, rz_rs,
    rw_ss, rw_rs, rwz_ss, rwz_rs,
):
    grp = lax.axis_index("grp")
    comp = lax.axis_index("comp")
    tp = lax.axis_index("tp")
    core = comp % 2
    x = (comp // 2) % 4
    z = comp // 8

    def device(dz, dx, dc):
        zz = 1 - z if dz else z
        cc = 1 - core if dc else core
        return (grp, zz * 8 + ((x + dx) % 4) * 2 + cc, tp)

    partner = device(1, 0, 0)
    barrier = pltpu.get_barrier_semaphore()
    pl.semaphore_signal(barrier, inc=1, device_id=partner, device_id_type=MESH)
    for dx, dc in NEAR:
        pl.semaphore_signal(barrier, inc=1, device_id=device(0, dx, dc), device_id_type=MESH)

    loads = [
        pltpu.make_async_copy(src, dst, in_sem.at[i])
        for i, (src, dst) in enumerate(
            [(pk_hbm, pk_in), (pv_hbm, pv_in), (q_hbm, q_in), (ck_hbm, ck_in), (up_hbm, up_in), (cv_hbm, cv_in)]
        )
    ]
    for load in loads:
        load.start()
    loads[0].wait()
    loads[1].wait()
    kv[0, 0, :, :D] = pk_in[...]
    kv[0, 0, :, D:] = pv_in[...]
    reward_own[...] = jnp.full((1, D), reward_ref[0], F32)

    for load in loads[2:]:
        load.wait()
    valid = lax.broadcasted_iota(jnp.int32, (ROWS, D), 0) < length_ref[0]
    for h in range(HEADS):
        block = slice(h * D, (h + 1) * D)
        qs[h * ROWS : (h + 1) * ROWS, :] = q_in[:, block]
        upstream = up_in[:, block]
        cs[h * ROWS : (h + 1) * ROWS, :] = jnp.where(valid, upstream, jnp.zeros_like(upstream))

    def scores_of(keys, values, row, chunk, mask):
        count = keys.shape[0]

        def one_head(h, _):
            at = pl.ds(pl.multiple_of(h * ROWS, ROWS), ROWS)
            s = mm_t(keys, qs[at, :]) * EXP2_SCALE
            d = mm_t(values, cs[at, :])
            if mask is not None:
                s = jnp.where(mask, s, -1e30)
            top = jnp.max(s, axis=0, keepdims=True)
            e = jnp.exp2(s - top)
            exps[row : row + count, at] = e
            dps[row : row + count, at] = d
            tops[chunk : chunk + 1, at] = top
            sums[chunk : chunk + 1, at] = jnp.sum(e, axis=0, keepdims=True)
            dots[chunk : chunk + 1, at] = jnp.sum(e * d, axis=0, keepdims=True)
            return 0

        lax.fori_loop(0, HEADS, one_head, 0, unroll=2)

    def pair_scores(half, dx):
        block = kv[half, 2 * dx : 2 * dx + 2].reshape(PAIR, 2 * D)
        chunk = half * 4 + dx
        scores_of(block[:, :D], block[:, D:], chunk * PAIR, chunk, None)

    key_pos = lax.broadcasted_iota(jnp.int32, (ROWS, ROWS), 0)
    query_pos = lax.broadcasted_iota(jnp.int32, (ROWS, ROWS), 1)
    scores_of(ck_in[...], cv_in[...], SPAN, CHUNKS - 1, key_pos <= query_pos)

    pl.semaphore_wait(barrier, len(NEAR) + 1)

    def send(src, dst, ss, rs, to):
        copy = pltpu.make_async_remote_copy(
            src_ref=src, dst_ref=dst, send_sem=ss, recv_sem=rs, device_id=to, device_id_type=MESH
        )
        copy.start()
        return copy

    z_copy = send(kv.at[0, 0], kv.at[1, 0], zkv_ss, zkv_rs, partner)
    rz_copy = send(reward_own, reward_z, rwz_ss, rwz_rs, partner)
    pending = [z_copy, rz_copy]

    def spread(source, dest, ss, rs):
        copies = {}
        for i, (dx, dc) in enumerate(NEAR):
            there = slot_of(-dx, dc)
            copies[there] = send(source(dx, dc), dest(there), ss.at[i], rs.at[there], device(0, dx, dc))
            pending.append(copies[there])
        return copies

    near = spread(lambda dx, dc: kv.at[0, 0], lambda s: kv.at[0, s], near_ss, near_rs)
    near[1].wait_recv()
    pair_scores(0, 0)
    for dx in (1, 3, 2):
        near[2 * dx].wait_recv()
        near[2 * dx + 1].wait_recv()
        pair_scores(0, dx)

    z_copy.wait_recv()
    far = spread(lambda dx, dc: kv.at[1, 0], lambda s: kv.at[1, s], far_ss, far_rs)
    rz_copy.wait_recv()
    reward_pair[...] = reward_own[...] + reward_z[...]
    reward_copies = spread(lambda dx, dc: reward_pair, lambda s: reward_recv.at[s], rw_ss, rw_rs)

    far[1].wait_recv()
    pair_scores(1, 0)
    for dx in (1, 3, 2):
        far[2 * dx].wait_recv()
        far[2 * dx + 1].wait_recv()
        pair_scores(1, dx)

    total = reward_pair[...]
    for there, copy in reward_copies.items():
        copy.wait_recv()
        total = total + reward_recv[there]
    advantage = reward_own[...] - total / 16.0

    top = tops[0:CHUNKS, :]
    factor = jnp.exp2(top - jnp.max(top, axis=0, keepdims=True))
    inverse = 1.0 / jnp.sum(sums[0:CHUNKS, :] * factor, axis=0, keepdims=True)
    factors[0:CHUNKS, :] = factor * inverse
    deltas[...] = jnp.sum(dots[0:CHUNKS, :] * factor, axis=0, keepdims=True) * inverse

    def grads_of(row, count, chunk):
        def one_head(h, _):
            at = pl.ds(pl.multiple_of(h * ROWS, ROWS), ROWS)
            p = exps[row : row + count, at] * factors[chunk : chunk + 1, at]
            ps[0:count, at] = p.astype(BF16)
            dss[row : row + count, at] = (p * (dps[row : row + count, at] - deltas[:, at])).astype(BF16)
            return 0

        lax.fori_loop(0, HEADS, one_head, 0, unroll=2)
        dkey = mm(dss[row : row + count, :], qs[...]) * (advantage * SCALE)
        dvalue = mm(ps[0:count, :], cs[...]) * advantage
        return dkey, dvalue

    def terms(half, sends, ss, rs, recv):
        copies = {}
        order = {pair: i for i, pair in enumerate(NEAR)}
        for dx in (2, 1, 3, 0):
            chunk = half * 4 + dx
            dkey, dvalue = grads_of(chunk * PAIR, PAIR, chunk)
            for dc in (0, 1):
                rows = slice(dc * SHARD, (dc + 1) * SHARD)
                if (dx, dc) == (0, 0):
                    own[half, :, :D] = dkey[rows]
                    own[half, :, D:] = dvalue[rows]
                    continue
                here, there = slot_of(dx, dc), slot_of(-dx, dc)
                sends[here, :, :D] = dkey[rows].astype(BF16)
                sends[here, :, D:] = dvalue[rows].astype(BF16)
                i = order[(dx, dc)]
                copies[there] = send(
                    sends.at[here], recv.at[there], ss.at[i], rs.at[there], device(0, dx, dc)
                )
                pending.append(copies[there])
        return copies

    def collect(half, copies, recv):
        result = own[half]
        for there, copy in copies.items():
            copy.wait_recv()
            result = result + recv[there].astype(F32)
        return result

    far_terms = terms(1, far_send, rfar_ss, rfar_rs, far_recv)
    near_terms = terms(0, near_send, rnear_ss, rnear_rs, near_recv)

    z_send[...] = collect(1, far_terms, far_recv).astype(BF16)
    z_terms = send(z_send, z_recv, rz_ss, rz_rs, partner)
    pending.append(z_terms)

    dkey, dvalue = grads_of(SPAN, ROWS, CHUNKS - 1)
    dck_out[...] = dkey.astype(BF16)
    dcv_out[...] = dvalue.astype(BF16)
    for half in (0, 1):
        for s in range(8):
            at = half * HALF + s * SHARD
            kt[at : at + SHARD, :] = kv[half, s, :, :D]
    kt[SPAN:, :] = ck_in[...]
    keys_t = kt[...].T
    for h in range(HEADS):
        dquery = mm(keys_t, dss[:, h * ROWS : (h + 1) * ROWS])
        dq_out[:, h * D : (h + 1) * D] = (dquery.T * (advantage * SCALE)).astype(BF16)
    stores = [
        pltpu.make_async_copy(dq_out, dq_hbm, out_sem.at[0]),
        pltpu.make_async_copy(dck_out, dck_hbm, out_sem.at[1]),
        pltpu.make_async_copy(dcv_out, dcv_hbm, out_sem.at[2]),
    ]
    for store in stores:
        store.start()

    near_sum = collect(0, near_terms, near_recv)
    z_terms.wait_recv()
    result = near_sum + z_recv[...].astype(F32)
    dpk_out[...] = result[:, :D].astype(BF16)
    dpv_out[...] = result[:, D:].astype(BF16)
    last = [
        pltpu.make_async_copy(dpk_out, dpk_hbm, out_sem.at[3]),
        pltpu.make_async_copy(dpv_out, dpv_hbm, out_sem.at[4]),
    ]
    for store in last:
        store.start()
    for copy in pending:
        copy.wait_send()
    for store in stores + last:
        store.wait()


def shards(queries, comp_keys, comp_values, prompt_keys, prompt_values, upstream, rewards, lengths):
    hbm = pl.BlockSpec(memory_space=pl.ANY)
    smem = pl.BlockSpec(memory_space=pltpu.SMEM)
    vmem = pltpu.VMEM
    dma = pltpu.SemaphoreType.DMA
    return pl.pallas_call(
        kernel,
        name="attention_backward",
        out_shape=[
            jax.ShapeDtypeStruct((ROWS, HEADS * D), BF16),
            jax.ShapeDtypeStruct((ROWS, D), BF16),
            jax.ShapeDtypeStruct((ROWS, D), BF16),
            jax.ShapeDtypeStruct((SHARD, D), BF16),
            jax.ShapeDtypeStruct((SHARD, D), BF16),
        ],
        in_specs=[hbm] * 6 + [smem] * 2,
        out_specs=[hbm] * 5,
        scratch_shapes=[
            vmem((ROWS, HEADS * D), BF16),
            vmem((ROWS, HEADS * D), BF16),
            vmem((ROWS, D), BF16),
            vmem((ROWS, D), BF16),
            vmem((SHARD, D), BF16),
            vmem((SHARD, D), BF16),
            vmem((ROWS, HEADS * D), BF16),
            vmem((ROWS, D), BF16),
            vmem((ROWS, D), BF16),
            vmem((SHARD, D), BF16),
            vmem((SHARD, D), BF16),
            vmem((COLS, D), BF16),
            vmem((COLS, D), BF16),
            vmem((2, 8, SHARD, 2 * D), BF16),
            vmem((KEYS, D), BF16),
            vmem((KEYS, COLS), F32),
            vmem((KEYS, COLS), F32),
            vmem((ROWS, COLS), BF16),
            vmem((KEYS, COLS), BF16),
            vmem((16, COLS), F32),
            vmem((16, COLS), F32),
            vmem((16, COLS), F32),
            vmem((16, COLS), F32),
            vmem((1, COLS), F32),
            vmem((2, SHARD, 2 * D), F32),
            vmem((8, SHARD, 2 * D), BF16),
            vmem((8, SHARD, 2 * D), BF16),
            vmem((8, SHARD, 2 * D), BF16),
            vmem((8, SHARD, 2 * D), BF16),
            vmem((SHARD, 2 * D), BF16),
            vmem((SHARD, 2 * D), BF16),
            vmem((1, D), F32),
            vmem((1, D), F32),
            vmem((1, D), F32),
            vmem((8, 1, D), F32),
            dma((6,)),
            dma((5,)),
            dma((7,)),
            dma((8,)),
            dma((7,)),
            dma((8,)),
            dma,
            dma,
            dma((7,)),
            dma((8,)),
            dma((7,)),
            dma((8,)),
            dma,
            dma,
            dma((7,)),
            dma((8,)),
            dma,
            dma,
        ],
        compiler_params=pltpu.CompilerParams(
            collective_id=0, has_side_effects=True, vmem_limit_bytes=58 * 2**20
        ),
    )(queries, comp_keys, comp_values, prompt_keys, prompt_values, upstream, rewards, lengths)


def solution(mesh):
    rows = P(("grp", "comp"), "tp")
    scalars = P(("grp", "comp"))
    return jax.shard_map(
        shards, mesh=mesh, in_specs=(rows,) * 6 + (scalars,) * 2, out_specs=(rows,) * 5, check_vma=False
    )
```

```python
import math

import jax
import jax.numpy as jnp
from jax import lax
from jax.experimental import pallas as pl
from jax.experimental.pallas import tpu as pltpu
from jax.sharding import PartitionSpec as P

D = 128
HEADS = 8
ROWS = 256
SHARD = 96
HALF = 8 * SHARD
SPAN = 2 * HALF
KEYS = SPAN + ROWS
OWN_CHUNK = 6
CHUNKS = 7
COLS = HEADS * ROWS
QUAD = 4 * SHARD
FIRST, REST, ALL = (0, 1), (1, 4), (0, 4)
SCALE = D ** (-0.5)
EXP2_SCALE = SCALE * math.log2(math.e)
F32 = jnp.float32
BF16 = jnp.bfloat16
MESH = pl.DeviceIdType.MESH
PEERS = (2, 1, 3)
KEY, VALUE = 0, 1


def mm(a, b):
    return jnp.dot(a, b, preferred_element_type=F32)


def mm_t(a, b):
    return lax.dot_general(a, b, (((1,), (1,)), ((), ())), preferred_element_type=F32)


def kernel(
    q_hbm, ck_hbm, cv_hbm, pk_hbm, pv_hbm, up_hbm, reward_hbm, length_hbm,
    dq_out, dckv_out, dpkv_out,
    q_in, up_in, ck_in, cv_in, pk_in, pv_in, reward_ref, length_ref,
    qs, cs, kv, kt, exps, dps, ps, dss, tops, sums, dots, factors, deltas,
    held, pair_send, pair_recv, row_send, row_recv, z_send, z_recv,
    reward_own, reward_z, reward_pair, reward_quad, reward_sib, reward_recv,
    in_sem, kv_ss, kv_rs, row_ss, row_rs, sum_ss, sum_rs, pair_ss, pair_rs, misc_ss, misc_rs,
):
    grp = lax.axis_index("grp")
    comp = lax.axis_index("comp")
    tp = lax.axis_index("tp")
    core = comp % 2
    x = (comp // 2) % 4
    z = comp // 8
    partner = (grp, (1 - z) * 8 + x * 2 + core, tp)
    sibling = (grp, z * 8 + x * 2 + 1 - core, tp)
    row = {dx: (grp, z * 8 + ((x + dx) % 4) * 2 + core, tp) for dx in PEERS}

    barrier = pltpu.get_barrier_semaphore()
    for peer in (partner, *row.values(), sibling):
        pl.semaphore_signal(barrier, inc=1, device_id=peer, device_id_type=MESH)

    loads = [
        pltpu.make_async_copy(src, dst, in_sem.at[i])
        for i, (src, dst) in enumerate(
            [
                (pk_hbm, pk_in), (pv_hbm, pv_in), (reward_hbm, reward_ref), (length_hbm, length_ref),
                (q_hbm, q_in), (ck_hbm, ck_in), (up_hbm, up_in), (cv_hbm, cv_in),
            ]
        )
    ]
    for load in loads:
        load.start()
    for load in loads[:4]:
        load.wait()
    kv[0, 0, 0, :, :D] = pk_in[...]
    kv[0, 0, 0, :, D:] = pv_in[...]
    reward_own[...] = jnp.full((1, D), reward_ref[0], F32)

    pl.semaphore_wait(barrier, 5)

    pending = []

    def send(src, dst, ss, rs, to):
        copy = pltpu.make_async_remote_copy(
            src_ref=src, dst_ref=dst, send_sem=ss, recv_sem=rs, device_id=to, device_id_type=MESH
        )
        copy.start()
        pending.append(copy)
        return copy

    def across(src, dst, i):
        return send(src, dst, misc_ss.at[i], misc_rs.at[i], partner)

    def spread(half):
        own = kv.at[half, 0, 0]
        along = {
            (4 - dx) % 4: send(
                own, kv.at[half, 0, (4 - dx) % 4], kv_ss.at[half, 0, dx], kv_rs.at[half, 0, (4 - dx) % 4], row[dx]
            )
            for dx in PEERS
        }
        beside = {0: send(own, kv.at[half, 1, 0], kv_ss.at[half, 1, 0], kv_rs.at[half, 1, 0], sibling)}
        return along, beside

    def forward(half, along, beside):
        for dx in (1, 3, 2):
            along[dx].wait_recv()
            beside[dx] = send(
                kv.at[half, 0, dx], kv.at[half, 1, dx], kv_ss.at[half, 1, dx], kv_rs.at[half, 1, dx], sibling
            )

    def scores_of(keys, values, at_row, chunk, mask=None):
        rows = slice(at_row, at_row + keys.shape[0])
        for h in range(HEADS):
            at = slice(h * ROWS, (h + 1) * ROWS)
            s = mm_t(keys, qs[at, :]) * EXP2_SCALE
            d = mm_t(values, cs[at, :])
            if mask is not None:
                s = jnp.where(mask, s, -1e30)
            top = jnp.max(s, axis=0, keepdims=True)
            e = jnp.exp2(s - top)
            exps[rows, at] = e
            dps[rows, at] = d
            tops[chunk : chunk + 1, at] = top
            sums[chunk : chunk + 1, at] = jnp.sum(e, axis=0, keepdims=True)
            dots[chunk : chunk + 1, at] = jnp.sum(e * d, axis=0, keepdims=True)

    def prompt_scores(half, parity, part, chunk):
        first, last = part
        block = kv[half, parity, first:last].reshape((last - first) * SHARD, 2 * D)
        scores_of(block[:, :D], block[:, D:], half * HALF + parity * QUAD + first * SHARD, chunk)

    kv_z = across(kv.at[0, 0, 0], kv.at[1, 0, 0], 0)
    reward_across = across(reward_own, reward_z, 1)
    along, beside = spread(0)

    for load in loads[4:]:
        load.wait()
    valid = lax.broadcasted_iota(jnp.int32, (ROWS, D), 0) < length_ref[0]
    for h in range(HEADS):
        block = slice(h * D, (h + 1) * D)
        qs[h * ROWS : (h + 1) * ROWS, :] = q_in[:, block]
        upstream = up_in[:, block]
        cs[h * ROWS : (h + 1) * ROWS, :] = jnp.where(valid, upstream, jnp.zeros_like(upstream))

    key_pos = lax.broadcasted_iota(jnp.int32, (ROWS, ROWS), 0)
    query_pos = lax.broadcasted_iota(jnp.int32, (ROWS, ROWS), 1)
    scores_of(ck_in[...], cv_in[...], SPAN, OWN_CHUNK, key_pos <= query_pos)

    forward(0, along, beside)
    prompt_scores(0, 0, ALL, 0)

    kv_z.wait_recv()
    near_beside = beside
    along, beside = spread(1)
    reward_across.wait_recv()
    reward_pair[...] = reward_own[...] + reward_z[...]
    reward_along = {
        (4 - dx) % 4: send(
            reward_pair, reward_recv.at[(4 - dx) % 4], row_ss.at[dx], row_rs.at[(4 - dx) % 4], row[dx]
        )
        for dx in PEERS
    }
    for copy in near_beside.values():
        copy.wait_recv()
    prompt_scores(0, 1, ALL, 1)
    prompt_scores(1, 0, FIRST, 2)
    beside[0].wait_recv()
    prompt_scores(1, 1, FIRST, 3)
    forward(1, along, beside)
    total = reward_pair[...]
    for dx, copy in reward_along.items():
        copy.wait_recv()
        total = total + reward_recv[dx]
    reward_quad[...] = total
    reward_beside = send(reward_quad, reward_sib, misc_ss.at[2], misc_rs.at[2], sibling)
    prompt_scores(1, 0, REST, 4)
    for dx in (1, 3, 2):
        beside[dx].wait_recv()
    prompt_scores(1, 1, REST, 5)

    reward_beside.wait_recv()
    advantage = reward_own[...] - (reward_quad[...] + reward_sib[...]) / 16.0

    top = tops[0:CHUNKS, :]
    factor = jnp.exp2(top - jnp.max(top, axis=0, keepdims=True))
    inverse = 1.0 / jnp.sum(sums[0:CHUNKS, :] * factor, axis=0, keepdims=True)
    factors[0:CHUNKS, :] = factor * inverse
    deltas[...] = jnp.sum(dots[0:CHUNKS, :] * factor, axis=0, keepdims=True) * inverse

    def value_terms(at_row, chunks, room):
        count = sum(size for _, size in chunks)
        for h in range(HEADS):
            at = slice(h * ROWS, (h + 1) * ROWS)
            start = 0
            for chunk, size in chunks:
                rows = slice(at_row + start, at_row + start + size)
                p = exps[rows, at] * factors[chunk : chunk + 1, at]
                ps[room, start : start + size, at] = p.astype(BF16)
                start += size
        return mm(ps[room, 0:count, :], cs[...]) * advantage

    def key_terms(at_row, chunks):
        count = sum(size for _, size in chunks)
        for h in range(HEADS):
            at = slice(h * ROWS, (h + 1) * ROWS)
            start = 0
            for chunk, size in chunks:
                rows = slice(at_row + start, at_row + start + size)
                p = exps[rows, at] * factors[chunk : chunk + 1, at]
                dss[rows, at] = (p * (dps[rows, at] - deltas[:, at])).astype(BF16)
                start += size
        return mm(dss[at_row : at_row + count, :], qs[...]) * (advantage * SCALE)

    def to_sibling(half, kind, block):
        for dx in range(4):
            pair_send[half, kind, dx] = block[dx * SHARD : (dx + 1) * SHARD].astype(BF16)
        return send(
            pair_send.at[half, kind], pair_recv.at[half, kind], pair_ss.at[half, kind], pair_rs.at[half, kind], sibling
        )

    def along_row(half, kind, copy):
        copy.wait_recv()
        copies = {}
        for dx in PEERS:
            both = held[half, kind, dx * SHARD : (dx + 1) * SHARD] + pair_recv[half, kind, dx].astype(F32)
            row_send[half, kind, dx] = both.astype(BF16)
            there = (4 - dx) % 4
            copies[there] = send(
                row_send.at[half, kind, dx], row_recv.at[half, kind, there],
                sum_ss.at[half, kind, dx], sum_rs.at[half, kind, there], row[dx],
            )
        return copies

    def collect(half, kind, copies):
        result = held[half, kind, 0:SHARD] + pair_recv[half, kind, 0].astype(F32)
        for dx, copy in copies.items():
            copy.wait_recv()
            result = result + row_recv[half, kind, dx].astype(F32)
        return result

    def to_partner(kind, copies):
        z_send[kind] = collect(1, kind, copies).astype(BF16)
        return across(z_send.at[kind], z_recv.at[kind], 3 + kind)

    even, odd = ((2, SHARD), (4, QUAD - SHARD)), ((3, SHARD), (5, QUAD - SHARD))
    value_pair = to_sibling(1, VALUE, value_terms(HALF + QUAD, odd, 0))
    held[1, VALUE] = value_terms(HALF, even, 1)
    key_pair = to_sibling(1, KEY, key_terms(HALF + QUAD, odd))
    value_rows = along_row(1, VALUE, value_pair)
    held[1, KEY] = key_terms(HALF, even)
    key_rows = along_row(1, KEY, key_pair)

    for half in (0, 1):
        for parity in (0, 1):
            start = half * HALF + parity * QUAD
            kt[start : start + QUAD, :] = kv[half, parity].reshape(QUAD, 2 * D)[:, :D]
    kt[SPAN:, :] = ck_in[...]
    dckv_out[:, D:] = value_terms(SPAN, ((OWN_CHUNK, ROWS),), 0).astype(BF16)
    dckv_out[:, :D] = key_terms(SPAN, ((OWN_CHUNK, ROWS),)).astype(BF16)
    z_value = to_partner(VALUE, value_rows)
    z_key = to_partner(KEY, key_rows)

    near_value_pair = to_sibling(0, VALUE, value_terms(QUAD, ((1, QUAD),), 0))
    near_key_pair = to_sibling(0, KEY, key_terms(QUAD, ((1, QUAD),)))
    held[0, VALUE] = value_terms(0, ((0, QUAD),), 1)
    held[0, KEY] = key_terms(0, ((0, QUAD),))
    near_value_rows = along_row(0, VALUE, near_value_pair)
    near_key_rows = along_row(0, KEY, near_key_pair)

    keys_t = kt[...].T
    for h in range(HEADS):
        dquery = mm(keys_t, dss[:, h * ROWS : (h + 1) * ROWS])
        dq_out[:, h * D : (h + 1) * D] = (dquery.T * (advantage * SCALE)).astype(BF16)

    near_value = collect(0, VALUE, near_value_rows)
    near_key = collect(0, KEY, near_key_rows)
    z_value.wait_recv()
    dpkv_out[:, D:] = (near_value + z_recv[VALUE].astype(F32)).astype(BF16)
    z_key.wait_recv()
    dpkv_out[:, :D] = (near_key + z_recv[KEY].astype(F32)).astype(BF16)
    for copy in pending:
        copy.wait_send()


def shards(queries, comp_keys, comp_values, prompt_keys, prompt_values, upstream, rewards, lengths):
    hbm = pl.BlockSpec(memory_space=pl.ANY)
    vmem = pltpu.VMEM
    dma = pltpu.SemaphoreType.DMA
    dquery, dcomp, dprompt = pl.pallas_call(
        kernel,
        name="attention_backward",
        out_shape=[
            vmem((ROWS, HEADS * D), BF16),
            vmem((ROWS, 2 * D), BF16),
            vmem((SHARD, 2 * D), BF16),
        ],
        in_specs=[hbm] * 8,
        out_specs=[pl.BlockSpec(memory_space=vmem)] * 3,
        scratch_shapes=[
            vmem((ROWS, HEADS * D), BF16),
            vmem((ROWS, HEADS * D), BF16),
            vmem((ROWS, D), BF16),
            vmem((ROWS, D), BF16),
            vmem((SHARD, D), BF16),
            vmem((SHARD, D), BF16),
            pltpu.SMEM((1,), F32),
            pltpu.SMEM((1,), jnp.int32),
            vmem((COLS, D), BF16),
            vmem((COLS, D), BF16),
            vmem((2, 2, 4, SHARD, 2 * D), BF16),
            vmem((KEYS, D), BF16),
            vmem((KEYS, COLS), F32),
            vmem((KEYS, COLS), F32),
            vmem((2, QUAD, COLS), BF16),
            vmem((KEYS, COLS), BF16),
            vmem((8, COLS), F32),
            vmem((8, COLS), F32),
            vmem((8, COLS), F32),
            vmem((8, COLS), F32),
            vmem((1, COLS), F32),
            vmem((2, 2, QUAD, D), F32),
            vmem((2, 2, 4, SHARD, D), BF16),
            vmem((2, 2, 4, SHARD, D), BF16),
            vmem((2, 2, 4, SHARD, D), BF16),
            vmem((2, 2, 4, SHARD, D), BF16),
            vmem((2, SHARD, D), BF16),
            vmem((2, SHARD, D), BF16),
            vmem((1, D), F32),
            vmem((1, D), F32),
            vmem((1, D), F32),
            vmem((1, D), F32),
            vmem((1, D), F32),
            vmem((4, 1, D), F32),
            dma((8,)),
            dma((2, 2, 4)),
            dma((2, 2, 4)),
            dma((4,)),
            dma((4,)),
            dma((2, 2, 4)),
            dma((2, 2, 4)),
            dma((2, 2)),
            dma((2, 2)),
            dma((6,)),
            dma((6,)),
        ],
        compiler_params=pltpu.CompilerParams(
            collective_id=0, has_side_effects=True, vmem_limit_bytes=56 * 2**20
        ),
    )(queries, comp_keys, comp_values, prompt_keys, prompt_values, upstream, rewards, lengths)
    return dquery, dcomp[:, :D], dcomp[:, D:], dprompt[:, :D], dprompt[:, D:]


def solution(mesh):
    rows = P(("grp", "comp"), "tp")
    scalars = P(("grp", "comp"))
    return jax.shard_map(
        shards, mesh=mesh, in_specs=(rows,) * 6 + (scalars,) * 2, out_specs=(rows,) * 5, check_vma=False
    )
```

```python
import math

import jax
import jax.numpy as jnp
from jax import lax
from jax.experimental import pallas as pl
from jax.experimental.pallas import tpu as pltpu
from jax.sharding import PartitionSpec as P

D = 128
HEADS = 8
ROWS = 256
SHARD = 96
HALF = 8 * SHARD
SPAN = 2 * HALF
KEYS = SPAN + ROWS
OWN_CHUNK = 6
CHUNKS = 7
COLS = HEADS * ROWS
QUAD = 4 * SHARD
FIRST, REST, ALL = (0, 1), (1, 4), (0, 4)
SCALE = D ** (-0.5)
EXP2_SCALE = SCALE * math.log2(math.e)
F32 = jnp.float32
BF16 = jnp.bfloat16
MESH = pl.DeviceIdType.MESH
PEERS = (2, 1, 3)
KEY, VALUE = 0, 1


def mm(a, b):
    return jnp.dot(a, b, preferred_element_type=F32)


def mm_t(a, b):
    return lax.dot_general(a, b, (((1,), (1,)), ((), ())), preferred_element_type=F32)


def kernel(
    q_hbm, ck_hbm, cv_hbm, pk_hbm, pv_hbm, up_hbm, reward_hbm, length_hbm,
    dq_out, dckv_out, dpkv_out,
    q_in, up_in, ck_in, cv_in, pk_in, pv_in, reward_ref, length_ref,
    qs, cs, kv, kt, exps, dps, ps, dss, tops, sums, dots, factors, deltas,
    held, pair_send, pair_recv, row_send, row_recv, z_send, z_recv,
    reward_own, reward_z, reward_pair, reward_quad, reward_sib, reward_recv,
    in_sem, kv_ss, kv_rs, row_ss, row_rs, sum_ss, sum_rs, pair_ss, pair_rs, misc_ss, misc_rs,
):
    grp = lax.axis_index("grp")
    comp = lax.axis_index("comp")
    tp = lax.axis_index("tp")
    core = comp % 2
    x = (comp // 2) % 4
    z = comp // 8
    partner = (grp, (1 - z) * 8 + x * 2 + core, tp)
    sibling = (grp, z * 8 + x * 2 + 1 - core, tp)
    row = {dx: (grp, z * 8 + ((x + dx) % 4) * 2 + core, tp) for dx in PEERS}

    barrier = pltpu.get_barrier_semaphore()
    for peer in (partner, *row.values(), sibling):
        pl.semaphore_signal(barrier, inc=1, device_id=peer, device_id_type=MESH)

    loads = [
        pltpu.make_async_copy(src, dst, in_sem.at[i])
        for i, (src, dst) in enumerate(
            [
                (pk_hbm, pk_in), (pv_hbm, pv_in), (reward_hbm, reward_ref), (length_hbm, length_ref),
                (q_hbm, q_in), (ck_hbm, ck_in), (up_hbm, up_in), (cv_hbm, cv_in),
            ]
        )
    ]
    for load in loads:
        load.start()
    for load in loads[:4]:
        load.wait()
    kv[0, 0, 0, :, :D] = pk_in[...]
    kv[0, 0, 0, :, D:] = pv_in[...]
    reward_own[...] = jnp.full((1, D), reward_ref[0], F32)

    pl.semaphore_wait(barrier, 5)

    pending = []

    def send(src, dst, ss, rs, to):
        copy = pltpu.make_async_remote_copy(
            src_ref=src, dst_ref=dst, send_sem=ss, recv_sem=rs, device_id=to, device_id_type=MESH
        )
        copy.start()
        pending.append(copy)
        return copy

    def across(src, dst, i):
        return send(src, dst, misc_ss.at[i], misc_rs.at[i], partner)

    def spread(half):
        own = kv.at[half, 0, 0]
        along = {
            (4 - dx) % 4: send(
                own, kv.at[half, 0, (4 - dx) % 4], kv_ss.at[half, 0, dx], kv_rs.at[half, 0, (4 - dx) % 4], row[dx]
            )
            for dx in PEERS
        }
        beside = {0: send(own, kv.at[half, 1, 0], kv_ss.at[half, 1, 0], kv_rs.at[half, 1, 0], sibling)}
        return along, beside

    def forward(half, along, beside):
        for dx in (1, 3, 2):
            along[dx].wait_recv()
            beside[dx] = send(
                kv.at[half, 0, dx], kv.at[half, 1, dx], kv_ss.at[half, 1, dx], kv_rs.at[half, 1, dx], sibling
            )

    def scores_of(keys, values, at_row, chunk, mask=None):
        rows = slice(at_row, at_row + keys.shape[0])
        for h in range(HEADS):
            at = slice(h * ROWS, (h + 1) * ROWS)
            s = mm_t(keys, qs[at, :]) * EXP2_SCALE
            d = mm_t(values, cs[at, :])
            if mask is not None:
                s = jnp.where(mask, s, -1e30)
            top = jnp.max(s, axis=0, keepdims=True)
            e = jnp.exp2(s - top)
            exps[rows, at] = e
            dps[rows, at] = d
            tops[chunk : chunk + 1, at] = top
            sums[chunk : chunk + 1, at] = jnp.sum(e, axis=0, keepdims=True)
            dots[chunk : chunk + 1, at] = jnp.sum(e * d, axis=0, keepdims=True)

    def prompt_scores(half, parity, part, chunk):
        first, last = part
        block = kv[half, parity, first:last].reshape((last - first) * SHARD, 2 * D)
        scores_of(block[:, :D], block[:, D:], half * HALF + parity * QUAD + first * SHARD, chunk)

    kv_z = across(kv.at[0, 0, 0], kv.at[1, 0, 0], 0)
    reward_across = across(reward_own, reward_z, 1)
    along, beside = spread(0)

    for load in loads[4:]:
        load.wait()
    valid = lax.broadcasted_iota(jnp.int32, (ROWS, D), 0) < length_ref[0]
    for h in range(HEADS):
        block = slice(h * D, (h + 1) * D)
        qs[h * ROWS : (h + 1) * ROWS, :] = q_in[:, block]
        upstream = up_in[:, block]
        cs[h * ROWS : (h + 1) * ROWS, :] = jnp.where(valid, upstream, jnp.zeros_like(upstream))

    key_pos = lax.broadcasted_iota(jnp.int32, (ROWS, ROWS), 0)
    query_pos = lax.broadcasted_iota(jnp.int32, (ROWS, ROWS), 1)
    scores_of(ck_in[...], cv_in[...], SPAN, OWN_CHUNK, key_pos <= query_pos)

    forward(0, along, beside)
    prompt_scores(0, 0, ALL, 0)

    kv_z.wait_recv()
    near_beside = beside
    along, beside = spread(1)
    reward_across.wait_recv()
    reward_pair[...] = reward_own[...] + reward_z[...]
    reward_along = {
        (4 - dx) % 4: send(
            reward_pair, reward_recv.at[(4 - dx) % 4], row_ss.at[dx], row_rs.at[(4 - dx) % 4], row[dx]
        )
        for dx in PEERS
    }
    for copy in near_beside.values():
        copy.wait_recv()
    prompt_scores(0, 1, ALL, 1)
    prompt_scores(1, 0, FIRST, 2)
    beside[0].wait_recv()
    prompt_scores(1, 1, FIRST, 3)
    forward(1, along, beside)
    total = reward_pair[...]
    for dx, copy in reward_along.items():
        copy.wait_recv()
        total = total + reward_recv[dx]
    reward_quad[...] = total
    reward_beside = send(reward_quad, reward_sib, misc_ss.at[2], misc_rs.at[2], sibling)
    prompt_scores(1, 0, REST, 4)
    for dx in (1, 3, 2):
        beside[dx].wait_recv()
    prompt_scores(1, 1, REST, 5)

    reward_beside.wait_recv()
    advantage = reward_own[...] - (reward_quad[...] + reward_sib[...]) / 16.0

    top = tops[0:CHUNKS, :]
    factor = jnp.exp2(top - jnp.max(top, axis=0, keepdims=True))
    inverse = 1.0 / jnp.sum(sums[0:CHUNKS, :] * factor, axis=0, keepdims=True)
    factors[0:CHUNKS, :] = factor * inverse
    deltas[...] = jnp.sum(dots[0:CHUNKS, :] * factor, axis=0, keepdims=True) * inverse

    def value_terms(at_row, count, chunk, room):
        rows = slice(at_row, at_row + count)
        for h in range(HEADS):
            at = slice(h * ROWS, (h + 1) * ROWS)
            ps[room, 0:count, at] = (exps[rows, at] * factors[chunk : chunk + 1, at]).astype(BF16)
        return mm(ps[room, 0:count, :], cs[...]) * advantage

    def key_terms(at_row, count, chunk, room):
        rows = slice(at_row, at_row + count)
        for h in range(HEADS):
            at = slice(h * ROWS, (h + 1) * ROWS)
            p = exps[rows, at] * factors[chunk : chunk + 1, at]
            dss[rows, at] = (p * (dps[rows, at] - deltas[:, at])).astype(BF16)
        return mm(dss[rows, :], qs[...]) * (advantage * SCALE)

    terms = {KEY: key_terms, VALUE: value_terms}

    def to_sibling(half, kind, part, chunk):
        first, last = part
        start = half * HALF + QUAD + first * SHARD
        block = terms[kind](start, (last - first) * SHARD, chunk, 0)
        for dx in range(first, last):
            pair_send[half, kind, dx] = block[(dx - first) * SHARD : (dx - first + 1) * SHARD].astype(BF16)
        i = 1 if first else 0
        return send(
            pair_send.at[half, kind, pl.ds(first, last - first)], pair_recv.at[half, kind, pl.ds(first, last - first)],
            pair_ss.at[half, kind, i], pair_rs.at[half, kind, i], sibling,
        )

    def hold(half, kind, part, chunk):
        first, last = part
        start = half * HALF + first * SHARD
        held[half, kind, first * SHARD : last * SHARD] = terms[kind](start, (last - first) * SHARD, chunk, 1)

    def along_row(half, kind, copy):
        copy.wait_recv()
        copies = {}
        for dx in PEERS:
            both = held[half, kind, dx * SHARD : (dx + 1) * SHARD] + pair_recv[half, kind, dx].astype(F32)
            row_send[half, kind, dx] = both.astype(BF16)
            there = (4 - dx) % 4
            copies[there] = send(
                row_send.at[half, kind, dx], row_recv.at[half, kind, there],
                sum_ss.at[half, kind, dx], sum_rs.at[half, kind, there], row[dx],
            )
        return copies

    def collect(half, kind, copies):
        result = held[half, kind, 0:SHARD] + pair_recv[half, kind, 0].astype(F32)
        for dx, copy in copies.items():
            copy.wait_recv()
            result = result + row_recv[half, kind, dx].astype(F32)
        return result

    def to_partner(kind, copies):
        z_send[kind] = collect(1, kind, copies).astype(BF16)
        return across(z_send.at[kind], z_recv.at[kind], 3 + kind)

    value_pair = to_sibling(1, VALUE, REST, 5)
    hold(1, VALUE, REST, 4)
    key_pair = to_sibling(1, KEY, REST, 5)
    value_rows = along_row(1, VALUE, value_pair)
    hold(1, KEY, REST, 4)
    key_rows = along_row(1, KEY, key_pair)
    value_first = to_sibling(1, VALUE, FIRST, 3)
    key_first = to_sibling(1, KEY, FIRST, 3)
    hold(1, VALUE, FIRST, 2)
    hold(1, KEY, FIRST, 2)

    for half in (0, 1):
        for parity in (0, 1):
            start = half * HALF + parity * QUAD
            kt[start : start + QUAD, :] = kv[half, parity].reshape(QUAD, 2 * D)[:, :D]
    kt[SPAN:, :] = ck_in[...]
    value_first.wait_recv()
    z_value = to_partner(VALUE, value_rows)
    key_first.wait_recv()
    z_key = to_partner(KEY, key_rows)

    near_value_pair = to_sibling(0, VALUE, ALL, 1)
    near_key_pair = to_sibling(0, KEY, ALL, 1)
    hold(0, VALUE, ALL, 0)
    hold(0, KEY, ALL, 0)
    near_value_rows = along_row(0, VALUE, near_value_pair)
    near_key_rows = along_row(0, KEY, near_key_pair)

    dckv_out[:, D:] = value_terms(SPAN, ROWS, OWN_CHUNK, 0).astype(BF16)
    dckv_out[:, :D] = key_terms(SPAN, ROWS, OWN_CHUNK, 0).astype(BF16)
    keys_t = kt[...].T
    for h in range(HEADS):
        dquery = mm(keys_t, dss[:, h * ROWS : (h + 1) * ROWS])
        dq_out[:, h * D : (h + 1) * D] = (dquery.T * (advantage * SCALE)).astype(BF16)

    near_value = collect(0, VALUE, near_value_rows)
    near_key = collect(0, KEY, near_key_rows)
    z_value.wait_recv()
    dpkv_out[:, D:] = (near_value + z_recv[VALUE].astype(F32)).astype(BF16)
    z_key.wait_recv()
    dpkv_out[:, :D] = (near_key + z_recv[KEY].astype(F32)).astype(BF16)
    for copy in pending:
        copy.wait_send()


def shards(queries, comp_keys, comp_values, prompt_keys, prompt_values, upstream, rewards, lengths):
    hbm = pl.BlockSpec(memory_space=pl.ANY)
    vmem = pltpu.VMEM
    dma = pltpu.SemaphoreType.DMA
    dquery, dcomp, dprompt = pl.pallas_call(
        kernel,
        name="attention_backward",
        out_shape=[
            vmem((ROWS, HEADS * D), BF16),
            vmem((ROWS, 2 * D), BF16),
            vmem((SHARD, 2 * D), BF16),
        ],
        in_specs=[hbm] * 8,
        out_specs=[pl.BlockSpec(memory_space=vmem)] * 3,
        scratch_shapes=[
            vmem((ROWS, HEADS * D), BF16),
            vmem((ROWS, HEADS * D), BF16),
            vmem((ROWS, D), BF16),
            vmem((ROWS, D), BF16),
            vmem((SHARD, D), BF16),
            vmem((SHARD, D), BF16),
            pltpu.SMEM((1,), F32),
            pltpu.SMEM((1,), jnp.int32),
            vmem((COLS, D), BF16),
            vmem((COLS, D), BF16),
            vmem((2, 2, 4, SHARD, 2 * D), BF16),
            vmem((KEYS, D), BF16),
            vmem((KEYS, COLS), F32),
            vmem((KEYS, COLS), F32),
            vmem((2, QUAD, COLS), BF16),
            vmem((KEYS, COLS), BF16),
            vmem((8, COLS), F32),
            vmem((8, COLS), F32),
            vmem((8, COLS), F32),
            vmem((8, COLS), F32),
            vmem((1, COLS), F32),
            vmem((2, 2, QUAD, D), F32),
            vmem((2, 2, 4, SHARD, D), BF16),
            vmem((2, 2, 4, SHARD, D), BF16),
            vmem((2, 2, 4, SHARD, D), BF16),
            vmem((2, 2, 4, SHARD, D), BF16),
            vmem((2, SHARD, D), BF16),
            vmem((2, SHARD, D), BF16),
            vmem((1, D), F32),
            vmem((1, D), F32),
            vmem((1, D), F32),
            vmem((1, D), F32),
            vmem((1, D), F32),
            vmem((4, 1, D), F32),
            dma((8,)),
            dma((2, 2, 4)),
            dma((2, 2, 4)),
            dma((4,)),
            dma((4,)),
            dma((2, 2, 4)),
            dma((2, 2, 4)),
            dma((2, 2, 2)),
            dma((2, 2, 2)),
            dma((6,)),
            dma((6,)),
        ],
        compiler_params=pltpu.CompilerParams(
            collective_id=0, has_side_effects=True, vmem_limit_bytes=56 * 2**20
        ),
    )(queries, comp_keys, comp_values, prompt_keys, prompt_values, upstream, rewards, lengths)
    return dquery, dcomp[:, :D], dcomp[:, D:], dprompt[:, :D], dprompt[:, D:]


def solution(mesh):
    rows = P(("grp", "comp"), "tp")
    scalars = P(("grp", "comp"))
    return jax.shard_map(
        shards, mesh=mesh, in_specs=(rows,) * 6 + (scalars,) * 2, out_specs=(rows,) * 5, check_vma=False
    )
```

```python
import math

import jax
import jax.numpy as jnp
from jax import lax
from jax.experimental import pallas as pl
from jax.experimental.pallas import tpu as pltpu
from jax.sharding import PartitionSpec as P

D = 128
HEADS = 8
ROWS = 256
SHARD = 96
HALF = 8 * SHARD
SPAN = 2 * HALF
KEYS = SPAN + ROWS
OWN_CHUNK = 6
CHUNKS = 7
COLS = HEADS * ROWS
QUAD = 4 * SHARD
FIRST, REST, ALL = (0, 1), (1, 4), (0, 4)
SCALE = D ** (-0.5)
EXP2_SCALE = SCALE * math.log2(math.e)
F32 = jnp.float32
BF16 = jnp.bfloat16
MESH = pl.DeviceIdType.MESH
PEERS = (2, 1, 3)
KEY, VALUE = 0, 1


def mm(a, b):
    return jnp.dot(a, b, preferred_element_type=F32)


def mm_t(a, b):
    return lax.dot_general(a, b, (((1,), (1,)), ((), ())), preferred_element_type=F32)


def kernel(
    q_hbm, ck_hbm, cv_hbm, pk_hbm, pv_hbm, up_hbm, reward_hbm, length_hbm,
    dq_out, dckv_out, dpkv_out,
    q_in, up_in, ck_in, cv_in, pk_in, pv_in, reward_ref, length_ref,
    qs, cs, kv, kt, exps, dps, ps, dss, tops, sums, dots, factors, deltas,
    held, pair_send, pair_recv, row_send, row_recv, z_send, z_recv,
    reward_own, reward_z, reward_pair, reward_quad, reward_sib, reward_recv,
    in_sem, kv_ss, kv_rs, row_ss, row_rs, sum_ss, sum_rs, pair_ss, pair_rs, misc_ss, misc_rs,
):
    grp = lax.axis_index("grp")
    comp = lax.axis_index("comp")
    tp = lax.axis_index("tp")
    core = comp % 2
    x = (comp // 2) % 4
    z = comp // 8
    partner = (grp, (1 - z) * 8 + x * 2 + core, tp)
    sibling = (grp, z * 8 + x * 2 + 1 - core, tp)
    row = {dx: (grp, z * 8 + ((x + dx) % 4) * 2 + core, tp) for dx in PEERS}

    barrier = pltpu.get_barrier_semaphore()
    for peer in (partner, *row.values(), sibling):
        pl.semaphore_signal(barrier, inc=1, device_id=peer, device_id_type=MESH)

    loads = [
        pltpu.make_async_copy(src, dst, in_sem.at[i])
        for i, (src, dst) in enumerate(
            [
                (pk_hbm, pk_in), (pv_hbm, pv_in), (reward_hbm, reward_ref), (length_hbm, length_ref),
                (q_hbm, q_in), (ck_hbm, ck_in), (up_hbm, up_in), (cv_hbm, cv_in),
            ]
        )
    ]
    for load in loads:
        load.start()
    for load in loads[:4]:
        load.wait()
    kv[0, 0, 0, :, :D] = pk_in[...]
    kv[0, 0, 0, :, D:] = pv_in[...]
    reward_own[...] = jnp.full((1, D), reward_ref[0], F32)

    pl.semaphore_wait(barrier, 5)

    pending = []

    def send(src, dst, ss, rs, to):
        copy = pltpu.make_async_remote_copy(
            src_ref=src, dst_ref=dst, send_sem=ss, recv_sem=rs, device_id=to, device_id_type=MESH
        )
        copy.start()
        pending.append(copy)
        return copy

    def across(src, dst, i):
        return send(src, dst, misc_ss.at[i], misc_rs.at[i], partner)

    def spread(half):
        own = kv.at[half, 0, 0]
        along = {
            (4 - dx) % 4: send(
                own, kv.at[half, 0, (4 - dx) % 4], kv_ss.at[half, 0, dx], kv_rs.at[half, 0, (4 - dx) % 4], row[dx]
            )
            for dx in PEERS
        }
        beside = {0: send(own, kv.at[half, 1, 0], kv_ss.at[half, 1, 0], kv_rs.at[half, 1, 0], sibling)}
        return along, beside

    def forward(half, along, beside):
        for dx in (1, 3, 2):
            along[dx].wait_recv()
            beside[dx] = send(
                kv.at[half, 0, dx], kv.at[half, 1, dx], kv_ss.at[half, 1, dx], kv_rs.at[half, 1, dx], sibling
            )

    def scores_of(keys, values, at_row, chunk, mask=None):
        rows = slice(at_row, at_row + keys.shape[0])
        for h in range(HEADS):
            at = slice(h * ROWS, (h + 1) * ROWS)
            s = mm_t(keys, qs[at, :]) * EXP2_SCALE
            d = mm_t(values, cs[at, :])
            if mask is not None:
                s = jnp.where(mask, s, -1e30)
            top = jnp.max(s, axis=0, keepdims=True)
            e = jnp.exp2(s - top)
            exps[rows, at] = e
            dps[rows, at] = d
            tops[chunk : chunk + 1, at] = top
            sums[chunk : chunk + 1, at] = jnp.sum(e, axis=0, keepdims=True)
            dots[chunk : chunk + 1, at] = jnp.sum(e * d, axis=0, keepdims=True)

    def prompt_scores(half, parity, part, chunk):
        first, last = part
        block = kv[half, parity, first:last].reshape((last - first) * SHARD, 2 * D)
        scores_of(block[:, :D], block[:, D:], half * HALF + parity * QUAD + first * SHARD, chunk)

    kv_z = across(kv.at[0, 0, 0], kv.at[1, 0, 0], 0)
    reward_across = across(reward_own, reward_z, 1)
    along, beside = spread(0)

    for load in loads[4:]:
        load.wait()
    valid = lax.broadcasted_iota(jnp.int32, (ROWS, D), 0) < length_ref[0]
    for h in range(HEADS):
        block = slice(h * D, (h + 1) * D)
        qs[h * ROWS : (h + 1) * ROWS, :] = q_in[:, block]
        upstream = up_in[:, block]
        cs[h * ROWS : (h + 1) * ROWS, :] = jnp.where(valid, upstream, jnp.zeros_like(upstream))

    key_pos = lax.broadcasted_iota(jnp.int32, (ROWS, ROWS), 0)
    query_pos = lax.broadcasted_iota(jnp.int32, (ROWS, ROWS), 1)
    scores_of(ck_in[...], cv_in[...], SPAN, OWN_CHUNK, key_pos <= query_pos)

    forward(0, along, beside)

    kv_z.wait_recv()
    near_beside = beside
    along, beside = spread(1)
    reward_across.wait_recv()
    reward_pair[...] = reward_own[...] + reward_z[...]
    reward_along = {
        (4 - dx) % 4: send(
            reward_pair, reward_recv.at[(4 - dx) % 4], row_ss.at[dx], row_rs.at[(4 - dx) % 4], row[dx]
        )
        for dx in PEERS
    }
    prompt_scores(0, 0, ALL, 0)
    for copy in near_beside.values():
        copy.wait_recv()
    prompt_scores(0, 1, ALL, 1)
    prompt_scores(1, 0, FIRST, 2)
    beside[0].wait_recv()
    prompt_scores(1, 1, FIRST, 3)
    forward(1, along, beside)
    total = reward_pair[...]
    for dx, copy in reward_along.items():
        copy.wait_recv()
        total = total + reward_recv[dx]
    reward_quad[...] = total
    reward_beside = send(reward_quad, reward_sib, misc_ss.at[2], misc_rs.at[2], sibling)
    prompt_scores(1, 0, REST, 4)
    for dx in (1, 3, 2):
        beside[dx].wait_recv()
    prompt_scores(1, 1, REST, 5)

    reward_beside.wait_recv()
    advantage = reward_own[...] - (reward_quad[...] + reward_sib[...]) / 16.0

    top = tops[0:CHUNKS, :]
    factor = jnp.exp2(top - jnp.max(top, axis=0, keepdims=True))
    inverse = 1.0 / jnp.sum(sums[0:CHUNKS, :] * factor, axis=0, keepdims=True)
    factors[0:CHUNKS, :] = factor * inverse
    deltas[...] = jnp.sum(dots[0:CHUNKS, :] * factor, axis=0, keepdims=True) * inverse

    def value_terms(at_row, count, chunk, room):
        rows = slice(at_row, at_row + count)
        for h in range(HEADS):
            at = slice(h * ROWS, (h + 1) * ROWS)
            ps[room, 0:count, at] = (exps[rows, at] * factors[chunk : chunk + 1, at]).astype(BF16)
        return mm(ps[room, 0:count, :], cs[...]) * advantage

    def key_terms(at_row, count, chunk, room):
        rows = slice(at_row, at_row + count)
        for h in range(HEADS):
            at = slice(h * ROWS, (h + 1) * ROWS)
            p = exps[rows, at] * factors[chunk : chunk + 1, at]
            dss[rows, at] = (p * (dps[rows, at] - deltas[:, at])).astype(BF16)
        return mm(dss[rows, :], qs[...]) * (advantage * SCALE)

    terms = {KEY: key_terms, VALUE: value_terms}

    def to_sibling(half, kind, part, chunk):
        first, last = part
        start = half * HALF + QUAD + first * SHARD
        block = terms[kind](start, (last - first) * SHARD, chunk, 0)
        for dx in range(first, last):
            pair_send[half, kind, dx] = block[(dx - first) * SHARD : (dx - first + 1) * SHARD].astype(BF16)
        i = 1 if first else 0
        return send(
            pair_send.at[half, kind, pl.ds(first, last - first)], pair_recv.at[half, kind, pl.ds(first, last - first)],
            pair_ss.at[half, kind, i], pair_rs.at[half, kind, i], sibling,
        )

    def hold(half, kind, part, chunk):
        first, last = part
        start = half * HALF + first * SHARD
        held[half, kind, first * SHARD : last * SHARD] = terms[kind](start, (last - first) * SHARD, chunk, 1)

    def along_row(half, kind, copy):
        copy.wait_recv()
        copies = {}
        for dx in PEERS:
            both = held[half, kind, dx * SHARD : (dx + 1) * SHARD] + pair_recv[half, kind, dx].astype(F32)
            row_send[half, kind, dx] = both.astype(BF16)
            there = (4 - dx) % 4
            copies[there] = send(
                row_send.at[half, kind, dx], row_recv.at[half, kind, there],
                sum_ss.at[half, kind, dx], sum_rs.at[half, kind, there], row[dx],
            )
        return copies

    def collect(half, kind, copies):
        result = held[half, kind, 0:SHARD] + pair_recv[half, kind, 0].astype(F32)
        for dx, copy in copies.items():
            copy.wait_recv()
            result = result + row_recv[half, kind, dx].astype(F32)
        return result

    def to_partner(kind, copies):
        z_send[kind] = collect(1, kind, copies).astype(BF16)
        return across(z_send.at[kind], z_recv.at[kind], 3 + kind)

    value_pair = to_sibling(1, VALUE, REST, 5)
    hold(1, VALUE, REST, 4)
    key_pair = to_sibling(1, KEY, REST, 5)
    value_rows = along_row(1, VALUE, value_pair)
    hold(1, KEY, REST, 4)
    key_rows = along_row(1, KEY, key_pair)
    value_first = to_sibling(1, VALUE, FIRST, 3)
    key_first = to_sibling(1, KEY, FIRST, 3)
    hold(1, VALUE, FIRST, 2)
    hold(1, KEY, FIRST, 2)

    for half in (0, 1):
        for parity in (0, 1):
            start = half * HALF + parity * QUAD
            kt[start : start + QUAD, :] = kv[half, parity].reshape(QUAD, 2 * D)[:, :D]
    kt[SPAN:, :] = ck_in[...]
    value_first.wait_recv()
    z_value = to_partner(VALUE, value_rows)
    key_first.wait_recv()
    z_key = to_partner(KEY, key_rows)

    near_value_pair = to_sibling(0, VALUE, ALL, 1)
    near_key_pair = to_sibling(0, KEY, ALL, 1)
    hold(0, VALUE, ALL, 0)
    hold(0, KEY, ALL, 0)
    near_value_rows = along_row(0, VALUE, near_value_pair)
    near_key_rows = along_row(0, KEY, near_key_pair)

    dckv_out[:, D:] = value_terms(SPAN, ROWS, OWN_CHUNK, 0).astype(BF16)
    dckv_out[:, :D] = key_terms(SPAN, ROWS, OWN_CHUNK, 0).astype(BF16)
    keys_t = kt[...].T
    for h in range(HEADS):
        dquery = mm(keys_t, dss[:, h * ROWS : (h + 1) * ROWS])
        dq_out[:, h * D : (h + 1) * D] = (dquery.T * (advantage * SCALE)).astype(BF16)

    near_value = collect(0, VALUE, near_value_rows)
    near_key = collect(0, KEY, near_key_rows)
    z_value.wait_recv()
    dpkv_out[:, D:] = (near_value + z_recv[VALUE].astype(F32)).astype(BF16)
    z_key.wait_recv()
    dpkv_out[:, :D] = (near_key + z_recv[KEY].astype(F32)).astype(BF16)
    for copy in pending:
        copy.wait_send()


def shards(queries, comp_keys, comp_values, prompt_keys, prompt_values, upstream, rewards, lengths):
    hbm = pl.BlockSpec(memory_space=pl.ANY)
    vmem = pltpu.VMEM
    dma = pltpu.SemaphoreType.DMA
    dquery, dcomp, dprompt = pl.pallas_call(
        kernel,
        name="attention_backward",
        out_shape=[
            vmem((ROWS, HEADS * D), BF16),
            vmem((ROWS, 2 * D), BF16),
            vmem((SHARD, 2 * D), BF16),
        ],
        in_specs=[hbm] * 8,
        out_specs=[pl.BlockSpec(memory_space=vmem)] * 3,
        scratch_shapes=[
            vmem((ROWS, HEADS * D), BF16),
            vmem((ROWS, HEADS * D), BF16),
            vmem((ROWS, D), BF16),
            vmem((ROWS, D), BF16),
            vmem((SHARD, D), BF16),
            vmem((SHARD, D), BF16),
            pltpu.SMEM((1,), F32),
            pltpu.SMEM((1,), jnp.int32),
            vmem((COLS, D), BF16),
            vmem((COLS, D), BF16),
            vmem((2, 2, 4, SHARD, 2 * D), BF16),
            vmem((KEYS, D), BF16),
            vmem((KEYS, COLS), F32),
            vmem((KEYS, COLS), F32),
            vmem((2, QUAD, COLS), BF16),
            vmem((KEYS, COLS), BF16),
            vmem((8, COLS), F32),
            vmem((8, COLS), F32),
            vmem((8, COLS), F32),
            vmem((8, COLS), F32),
            vmem((1, COLS), F32),
            vmem((2, 2, QUAD, D), F32),
            vmem((2, 2, 4, SHARD, D), BF16),
            vmem((2, 2, 4, SHARD, D), BF16),
            vmem((2, 2, 4, SHARD, D), BF16),
            vmem((2, 2, 4, SHARD, D), BF16),
            vmem((2, SHARD, D), BF16),
            vmem((2, SHARD, D), BF16),
            vmem((1, D), F32),
            vmem((1, D), F32),
            vmem((1, D), F32),
            vmem((1, D), F32),
            vmem((1, D), F32),
            vmem((4, 1, D), F32),
            dma((8,)),
            dma((2, 2, 4)),
            dma((2, 2, 4)),
            dma((4,)),
            dma((4,)),
            dma((2, 2, 4)),
            dma((2, 2, 4)),
            dma((2, 2, 2)),
            dma((2, 2, 2)),
            dma((6,)),
            dma((6,)),
        ],
        compiler_params=pltpu.CompilerParams(
            collective_id=0, has_side_effects=True, vmem_limit_bytes=56 * 2**20
        ),
    )(queries, comp_keys, comp_values, prompt_keys, prompt_values, upstream, rewards, lengths)
    return dquery, dcomp[:, :D], dcomp[:, D:], dprompt[:, :D], dprompt[:, D:]


def solution(mesh):
    rows = P(("grp", "comp"), "tp")
    scalars = P(("grp", "comp"))
    return jax.shard_map(
        shards, mesh=mesh, in_specs=(rows,) * 6 + (scalars,) * 2, out_specs=(rows,) * 5, check_vma=False
    )
```
